128 devices in a mesh: rep: 4 (over z), fsdp: 32 (over x, y, core).
Axes of the slice: x: 4, y: 4, z: 4, core: 2. Of those that a mesh axis runs over, the one named last changes fastest.
Arguments:
- grads: bfloat16 [4, 4096, 16384], P('rep', 'fsdp'), may hold values from -12 to 12
- slot_blocks: int32 [256], replicated, may hold values from 0 to 255, as said below
- basis_left: bfloat16 [256, 512, 512], P(('rep', 'fsdp'))
- basis_right: bfloat16 [256, 512, 512], P(('rep', 'fsdp'))
- stat_left: float32 [256, 512, 512], P(('rep', 'fsdp')), as said below
- stat_right: float32 [256, 512, 512], P(('rep', 'fsdp')), as said below
- moment: bfloat16 [256, 512, 512], P(('rep', 'fsdp')), may hold values from -6 to 6
- second: bfloat16 [256, 512, 512], P(('rep', 'fsdp')), may hold values from 0.25 to 4
Outputs:
- update: bfloat16 [4096, 16384], P('fsdp')
- basis_left_new: bfloat16 [256, 512, 512], P(('rep', 'fsdp'))
- basis_right_new: bfloat16 [256, 512, 512], P(('rep', 'fsdp'))
- stat_left_new: float32 [256, 512, 512], P(('rep', 'fsdp'))
- stat_right_new: float32 [256, 512, 512], P(('rep', 'fsdp'))
- moment_new: bfloat16 [256, 512, 512], P(('rep', 'fsdp'))
- second_new: bfloat16 [256, 512, 512], P(('rep', 'fsdp'))
The draws below stay inside these ranges and needn't reach their ends.
Inputs may be any that keep to these rules, and one draw needn't show every extreme that they name: `slot_blocks`: entry s names the block held in slot s % 2 of the device of index s // 2 along rep+fsdp. Every block appears once, and in every block row exactly 1 block are held by devices of each fsdp index. `stat_left`: every block is symmetric positive definite. `stat_right`: every block is symmetric positive definite.
All inputs are finite; a program needn't handle non-finite values.
Results may differ from the reference program's by a relative error of at most 0.012.
Values may be sent and summed in bfloat16 or wider, within the bound.
No kernel may reach another device: no remote copies, remote signals or barrier semaphores. Data moves between devices by JAX's collectives and lax.ppermute only.
A program may use at most 192 MiB of HBM per device.

```python
import math
import jax
import jax.numpy as jnp
from jax import lax

D_WIN = 4096
FF_WIN = 16384
BLK = 512
BR = 8
BC = 32
BLOCKS = 256
SLOTS = 2
PER_COL = 1
N_REP = 4
N_FSDP = 32


def draw_slot_blocks(key, part):
    key = jax.random.fold_in(key, 11)
    row_key, slot_key = jax.random.split(key)
    row_orders = jax.vmap(lambda sub_key: jax.random.permutation(sub_key, BC))(jax.random.split(row_key, BR))
    block_ids = jnp.arange(BR, dtype=jnp.int32)[:, None] * BC + row_orders.astype(jnp.int32)
    by_column = block_ids.reshape(BR, N_FSDP, PER_COL).transpose(1, 0, 2).reshape(N_FSDP, BR * PER_COL)
    shuffles = jax.vmap(lambda sub_key: jax.random.permutation(sub_key, BR * PER_COL))(jax.random.split(slot_key, N_FSDP))
    placed = jnp.take_along_axis(by_column, shuffles.astype(jnp.int32), axis=1)
    return placed.reshape(N_FSDP, N_REP, SLOTS).transpose(1, 0, 2).reshape(BLOCKS).astype(jnp.int32)


def near_identity(sign_key, noise_part):
    sign_values = 2.0 * jax.random.randint(sign_key, (BLOCKS, BLK), 0, 2).astype(jnp.float32) - 1.0
    return noise_part + jnp.eye(BLK, dtype=jnp.float32)[None] * sign_values[:, None, :]


def symmetric(diagonal_part, noise_part):
    mirrored = (noise_part + jnp.swapaxes(noise_part, 1, 2)) * 0.70710678
    return mirrored + jnp.eye(BLK, dtype=jnp.float32)[None] * diagonal_part[:, None, :]


def draw_basis_left(key, part):
    key = jax.random.fold_in(key, 21)
    sign_key, noise_key = jax.random.split(key)
    noise_part = 0.015 * jnp.clip(jax.random.normal(noise_key, (BLOCKS, BLK, BLK), jnp.float32), -4.0, 4.0)
    return near_identity(sign_key, noise_part).astype(jnp.bfloat16)


def draw_basis_right(key, part):
    key = jax.random.fold_in(key, 22)
    sign_key, noise_key = jax.random.split(key)
    noise_part = 0.015 * jnp.clip(jax.random.normal(noise_key, (BLOCKS, BLK, BLK), jnp.float32), -4.0, 4.0)
    return near_identity(sign_key, noise_part).astype(jnp.bfloat16)


def draw_stat_left(key, part):
    key = jax.random.fold_in(key, 31)
    diagonal_key, noise_key = jax.random.split(key)
    diagonal_part = jax.random.uniform(diagonal_key, (BLOCKS, BLK), jnp.float32, 24.0, 40.0)
    noise_part = 0.25 * jnp.clip(jax.random.normal(noise_key, (BLOCKS, BLK, BLK), jnp.float32), -3.0, 3.0)
    return symmetric(diagonal_part, noise_part)


def draw_stat_right(key, part):
    key = jax.random.fold_in(key, 32)
    diagonal_key, noise_key = jax.random.split(key)
    diagonal_part = jax.random.uniform(diagonal_key, (BLOCKS, BLK), jnp.float32, 24.0, 40.0)
    noise_part = 0.25 * jnp.clip(jax.random.normal(noise_key, (BLOCKS, BLK, BLK), jnp.float32), -3.0, 3.0)
    return symmetric(diagonal_part, noise_part)


def level_of(rng, shape, shards, smallest, top_value):
    loudness, own = 1.0, jax.random.fold_in(rng, 6)
    for axis_at, blocks in shards:
        heights = jnp.exp(jax.random.uniform(jax.random.fold_in(own, axis_at), (blocks,), jnp.float32, smallest / len(shards), top_value / len(shards)))
        loudness = loudness * jnp.repeat(heights, shape[axis_at] // blocks).reshape([-1 if axis == axis_at else 1 for axis in range(len(shape))])
    return loudness


def normal_values(key, shape, spread, limit, shards=(), kind=jnp.bfloat16):
    result = spread * jax.random.normal(key, shape, jnp.float32)
    if shards:
        result = result * level_of(key, shape, shards, -0.22, 0.18)
    return jnp.clip(result, -limit, limit).astype(kind)


def setup_inputs(seed: int = 0) -> dict:
    keys = jax.random.split(jax.random.key(seed), 9)
    grads = normal_values(keys[0], (N_REP, D_WIN, FF_WIN), 2.0, 12.0, ((0, 4), (1, 32)))
    slot_blocks = draw_slot_blocks(jax.random.fold_in(keys[8], 71), 0)
    basis_left = draw_basis_left(jax.random.fold_in(keys[8], 71), 0)
    basis_right = draw_basis_right(jax.random.fold_in(keys[8], 71), 0)
    stat_left = draw_stat_left(jax.random.fold_in(keys[8], 71), 0)
    stat_right = draw_stat_right(jax.random.fold_in(keys[8], 71), 0)
    moment = normal_values(keys[6], (BLOCKS, BLK, BLK), 1.0, 6.0, ((0, 128),))
    second = jnp.clip(jnp.exp(math.log(4.0) - 2.7725887 * jax.random.uniform(keys[7], (BLOCKS, BLK, BLK), jnp.float32) ** level_of(keys[7], (BLOCKS, BLK, BLK), ((0, 128),), -0.2, 0.2)), 0.25, 4.0).astype(jnp.bfloat16)
    return dict(grads=grads, slot_blocks=slot_blocks, basis_left=basis_left, basis_right=basis_right, stat_left=stat_left, stat_right=stat_right, moment=moment, second=second)


BETA_STAT = 0.95
BETA_ONE = 0.9
BETA_TWO = 0.95
EPSILON = 1e-08

def orthonormal(statistic, basis):
    highest = lax.Precision.HIGHEST
    power = jnp.dot(statistic.astype(jnp.float32), basis.astype(jnp.float32), precision=highest, preferred_element_type=jnp.float32)
    gram_matrix = jnp.dot(power.T.astype(jnp.float32), power.astype(jnp.float32), precision=highest, preferred_element_type=jnp.float32)
    factor = jnp.linalg.cholesky(gram_matrix)
    solved = lax.linalg.triangular_solve(factor, power, left_side=False, lower=True, transpose_a=True)
    return solved.astype(jnp.bfloat16)

def refine(gradient, left_basis, right_basis, left_stat, right_stat, first_moment, second_moment):
    highest = lax.Precision.HIGHEST
    left_new = BETA_STAT * left_stat + (1.0 - BETA_STAT) * jnp.dot(gradient.astype(jnp.float32), gradient.T.astype(jnp.float32), precision=highest, preferred_element_type=jnp.float32)
    right_new = BETA_STAT * right_stat + (1.0 - BETA_STAT) * jnp.dot(gradient.T.astype(jnp.float32), gradient.astype(jnp.float32), precision=highest, preferred_element_type=jnp.float32)
    first_new = (BETA_ONE * first_moment.astype(jnp.float32) + (1.0 - BETA_ONE) * gradient).astype(jnp.bfloat16)
    grad_low = gradient.astype(jnp.bfloat16)
    half_grad = jnp.dot(left_basis.T.astype(jnp.float32), grad_low.astype(jnp.float32), preferred_element_type=jnp.float32).astype(jnp.bfloat16)
    rotated_grad = jnp.dot(half_grad.astype(jnp.float32), right_basis.astype(jnp.float32), preferred_element_type=jnp.float32)
    half_moment = jnp.dot(left_basis.T.astype(jnp.float32), first_new.astype(jnp.float32), preferred_element_type=jnp.float32).astype(jnp.bfloat16)
    rotated_moment = jnp.dot(half_moment.astype(jnp.float32), right_basis.astype(jnp.float32), preferred_element_type=jnp.float32)
    second_wide = BETA_TWO * second_moment.astype(jnp.float32) + (1.0 - BETA_TWO) * rotated_grad * rotated_grad
    scaled = (rotated_moment / (jnp.sqrt(second_wide) + EPSILON)).astype(jnp.bfloat16)
    half_back = jnp.dot(left_basis.astype(jnp.float32), scaled.astype(jnp.float32), preferred_element_type=jnp.float32).astype(jnp.bfloat16)
    update_block = jnp.dot(half_back.astype(jnp.float32), right_basis.T.astype(jnp.float32), preferred_element_type=jnp.float32).astype(jnp.bfloat16)
    return (update_block, orthonormal(left_new, left_basis), orthonormal(right_new, right_basis), left_new, right_new, first_new, second_wide.astype(jnp.bfloat16))

def reference(grads, slot_blocks, basis_left, basis_right, stat_left, stat_right, moment, second):
    summed = grads[0].astype(jnp.float32)
    for group in range(1, N_REP):
        summed = summed + grads[group].astype(jnp.float32)
    mean_grad = summed / N_REP
    tiles = mean_grad.reshape(BR, BLK, BC, BLK).transpose(0, 2, 1, 3).reshape(BLOCKS, BLK, BLK)
    owned = jnp.take(tiles, slot_blocks, axis=0)
    results = lax.map(lambda entries: refine(*entries), (owned, basis_left, basis_right, stat_left, stat_right, moment, second))
    placed = jnp.zeros((BLOCKS, BLK, BLK), jnp.bfloat16).at[slot_blocks].set(results[0])
    update = placed.reshape(BR, BC, BLK, BLK).transpose(0, 2, 1, 3).reshape(D_WIN, FF_WIN)
    return (update, results[1], results[2], results[3], results[4], results[5], results[6])
```

```python
import jax
import jax.numpy as jnp
from jax import lax
from jax.experimental import pallas as pl
from jax.experimental.pallas import tpu as pltpu
from jax.sharding import PartitionSpec as P

BETA_STAT = 0.95
BETA_ONE = 0.9
BETA_TWO = 0.95
EPSILON = 1e-08
MIB = 1024 * 1024
NT = 128
SUB = 8

f32 = jnp.float32
bf16 = jnp.bfloat16
VM = pl.BlockSpec(memory_space=pltpu.VMEM)
SM = pl.BlockSpec(memory_space=pltpu.SMEM)
HBM = pl.BlockSpec(memory_space=pl.ANY)


def shape(dims, kind=bf16):
    return jax.ShapeDtypeStruct(dims, kind)


def params(limit):
    return pltpu.CompilerParams(vmem_limit_bytes=limit * MIB)


def cost(us, nbytes=MIB):
    return pl.CostEstimate(flops=int(us * 1e9), bytes_accessed=nbytes, transcendentals=0)


def around(step, size):
    return [(i, (i + step) % size) for i in range(size)]


def spread_kernel(pos, me, own, top_a, top_b, low_a, low_b, out):
    count, rows, width = out.shape
    half = rows // 2

    def move(d, _):
        at = pl.ds(pl.multiple_of(pos[d] * width, width), width)
        top = own[:half, at].astype(f32) + top_a[:, at].astype(f32) + top_b[:, at].astype(f32)
        low = own[half:, at].astype(f32) + low_a[:, at].astype(f32) + low_b[:, at].astype(f32)
        out[d, :half, :] = (top * 0.25).astype(bf16)
        out[d, half:, :] = (low * 0.25).astype(bf16)
        return 0

    lax.fori_loop(0, count, move, 0)


def pick_kernel(rows_of, me, received, *outs):
    reps = len(outs)
    for r in range(reps):
        k = lax.rem(me[0] + r, reps)
        for s in range(outs[r].shape[0]):
            outs[r][s] = received[rows_of[k, s]]


def unpick_kernel(rows_of, me, *refs):
    pieces, out = refs[:-1], refs[-1]
    reps = len(pieces)
    for r in range(reps):
        k = lax.rem(me[0] + r, reps)
        for s in range(pieces[r].shape[0]):
            out[rows_of[k, s]] = pieces[r][s]


def unspread_kernel(pos, received, out):
    count, rows, width = received.shape

    def move(d, _):
        out[:, pl.ds(pl.multiple_of(pos[d] * width, width), width)] = received[d]
        return 0

    lax.fori_loop(0, count, move, 0)


def dot(a, b, left=1, right=0):
    return lax.dot_general(a, b, (((left,), (right,)), ((), ())), preferred_element_type=f32)


def update_kernel(me, p0, p1, p2, p3, bl_ref, br_ref, moment, second, g_ref, moment_new, second_new, *rest):
    outs, full = rest[:-1], rest[-1]
    pieces = (p0, p1, p2, p3)
    reps = len(pieces)
    slots, side, _ = g_ref.shape
    strips = 4
    part = side // strips // reps
    for s in range(slots):
        for r in range(reps):
            q = lax.rem(me[0] + r, reps)
            for t in range(strips):
                at = pl.multiple_of(t * part * reps + q * part, part)
                g_ref[s, pl.ds(at, part), :] = pieces[r][s, t * part:(t + 1) * part, :]
    for s in range(slots):
        g, bl, br = g_ref[s], bl_ref[s], br_ref[s]
        first = (BETA_ONE * moment[s].astype(f32) + (1.0 - BETA_ONE) * g.astype(f32)).astype(bf16)
        moment_new[s] = first
        rotated_grad = dot(dot(bl, g, 0, 0).astype(bf16), br)
        rotated_moment = dot(dot(bl, first, 0, 0).astype(bf16), br)
        wide = BETA_TWO * second[s].astype(f32) + (1.0 - BETA_TWO) * rotated_grad * rotated_grad
        second_new[s] = wide.astype(bf16)
        scaled = (rotated_moment / (jnp.sqrt(wide) + EPSILON)).astype(bf16)
        full[...] = dot(dot(bl, scaled).astype(bf16), br, 1, 1).astype(bf16)
        for r in range(reps):
            q = lax.rem(me[0] + r, reps)
            for t in range(strips):
                at = pl.multiple_of(t * part * reps + q * part, part)
                outs[r][s, t * part:(t + 1) * part, :] = full[pl.ds(at, part), :]


def split3(a):
    hi = a.astype(bf16)
    rest = a - hi.astype(f32)
    mid = rest.astype(bf16)
    return hi, mid, (rest - mid.astype(f32)).astype(bf16)


def stat_kernel(g_ref, bl_ref, br_ref, sl_ref, sr_ref, sl_new, sr_new, power, gram):
    g = g_ref[0]
    for side, (old, new, basis, axis) in enumerate(((sl_ref, sl_new, bl_ref, 1), (sr_ref, sr_new, br_ref, 0))):
        stat = BETA_STAT * old[0] + (1.0 - BETA_STAT) * dot(g, g, axis, axis)
        new[0] = stat
        hi, mid, low = split3(stat)
        b = basis[0]
        p = dot(hi, b) + (dot(mid, b) + dot(low, b))
        power[side] = p
        gram[side] = exact_dot(p, p, 0, 0)


def exact_dot(a, b, left=1, right=0):
    return lax.dot_general(a, b, (((left,), (right,)), ((), ())), precision=lax.Precision.HIGHEST, preferred_element_type=f32)


def lane_column(block, lane):
    return jnp.broadcast_to(block[:, lane:lane + 1], block.shape)


def row_of(block, row):
    return jnp.broadcast_to(block[row:row + 1, :], block.shape)


def inverse_factors(work, out, count):
    lane = lax.broadcasted_iota(jnp.int32, (SUB, NT), 1)
    row = lax.broadcasted_iota(jnp.int32, (SUB, NT), 0)
    panels = [work[m, 0:SUB, :] for m in range(count)]
    for t in range(NT // SUB):
        first = t * SUB
        own = (lane >= first) & (lane < first + SUB)
        unit = (lane == first + row).astype(f32)
        cols, body, fwd, piv = [], [], [], []
        for m in range(count):
            cols.append([lane_column(panels[m], first + b) for b in range(SUB)])
            body.append(jnp.where(own, unit, panels[m]))
            fwd.append(body[m])
            piv.append(cols[m][0])
        for b in range(SUB):
            here = row == b
            for m in range(count):
                if b:
                    fwd[m] = jnp.where(here, body[m], fwd[m])
                    piv[m] = jnp.where(here, cols[m][b], piv[m])
                pivot = row_of(cols[m][b], b)
                inv = pl.reciprocal(pivot, approx=True)
                inv = inv * (2.0 - pivot * inv)
                inv = inv * (2.0 - pivot * inv)
                factor = jnp.where(here, -1.0, cols[m][b])
                scaled = factor * inv
                body[m] = jnp.where(here, 0.0, body[m]) - scaled * row_of(body[m], b)
                for c in range(b + 1, SUB):
                    cols[m][c] = jnp.where(here, 0.0, cols[m][c]) - scaled * row_of(cols[m][c], b)
        nxt = []
        spread = [[row_of(body[m], b) for b in range(SUB)] for m in range(count)]
        for u in range(t + 1, NT // SUB):
            for m in range(count):
                rows = work[m, u * SUB:(u + 1) * SUB, :]
                total = jnp.where(own, 0.0, rows)
                for b in range(SUB):
                    total = total - lane_column(rows, first + b) * spread[m][b]
                if u == t + 1:
                    nxt.append(total)
                else:
                    work[m, u * SUB:(u + 1) * SUB, :] = total
        for m in range(count):
            root = lax.rsqrt(piv[m])
            root = root * (1.5 - 0.5 * piv[m] * root * root)
            out[m, first:first + SUB, :] = jnp.where(lane < first + SUB, fwd[m] * root, 0.0)
        panels = nxt


def factor_kernel(steps, last, a_hbm, p_hbm, *refs):
    count, side, _ = a_hbm.shape
    done = steps * NT
    if last:
        early, left_out, right_out, a, p, work, inv, sem = refs
        for m in range(count):
            (left_out, right_out)[m % 2][m // 2, :, :done] = early[m]
    else:
        x_out, a_out, p_out, a, p, work, inv, sem = refs
    copies = [pltpu.make_async_copy(a_hbm, a, sem.at[0]), pltpu.make_async_copy(p_hbm, p, sem.at[1])]
    for copy in copies:
        copy.start()
    for copy in copies:
        copy.wait()

    def step(k, _):
        at = pl.multiple_of(k * NT, NT)
        for m in range(count):
            work[m] = a[m, pl.ds(at, NT), pl.ds(at, NT)]
        inverse_factors(work, inv, count)
        for kk in range(steps):

            @pl.when(k == kk)
            def _():
                lo, hi = kk * NT, (kk + 1) * NT
                for m in range(count):
                    w = inv[m]
                    x = exact_dot(p[m, :, lo:hi], w, 1, 1)
                    if last:
                        (left_out, right_out)[m % 2][m // 2, :, done + lo:done + hi] = x.astype(bf16)
                    else:
                        x_out[m, :, lo:hi] = x.astype(bf16)
                    if hi < side:
                        u = exact_dot(w, a[m, lo:hi, hi:])
                        a[m, hi:, hi:] = a[m, hi:, hi:] - exact_dot(u, u, 0, 0)
                        p[m, :, hi:] = p[m, :, hi:] - exact_dot(x, u)

        return 0

    lax.fori_loop(0, steps, step, 0)
    if not last:
        for m in range(count):
            a_out[m] = a[m, done:, done:]
            p_out[m] = p[m, :, done:]


def factor_call(last, name, outs, ins, specs):
    count, side, _ = ins[0].shape
    rows = ins[1].shape[1]
    scratch = [pltpu.VMEM((count, side, side), f32), pltpu.VMEM((count, rows, side), f32)]
    scratch += [pltpu.VMEM((count, NT, NT), f32)] * 2 + [pltpu.SemaphoreType.DMA((2,))]
    return call(lambda *refs: factor_kernel(2, last, *refs), outs, ins, specs, 50, cost(25, 12 * MIB), name, scratch)


def factor_first(a, p):
    count, side, _ = a.shape
    rest = side - 2 * NT
    outs = [shape((count, side, 2 * NT)), shape((count, rest, rest), f32), shape((count, side, rest), f32)]
    return factor_call(False, "factor_first", outs, (a, p), [HBM, HBM])


def factor_last(a, p, early):
    count, rows, _ = p.shape
    outs = [shape((count // 2, rows, rows))] * 2
    return factor_call(True, "factor_last", outs, (a, p, early), [HBM, HBM, VM])


def call(kernel, outs, ins, specs, limit, est, name, scratch=(), **extra):
    return pl.pallas_call(
        kernel, out_shape=outs, in_specs=specs, out_specs=[VM] * len(outs), scratch_shapes=list(scratch),
        compiler_params=params(limit), cost_estimate=est, name=name, **extra)(*ins)


def on_device(grads, slot_blocks, basis_left, basis_right, stat_left, stat_right, moment, second):
    fsdp = lax.axis_size("fsdp")
    reps = lax.axis_size("rep")
    slots, side, _ = basis_left.shape
    _, rows, columns = grads.shape
    block_cols = columns // side
    strips = side // rows
    part = rows // reps
    half = part // 2
    f = lax.axis_index("fsdp")
    rep = lax.axis_index("rep")
    me = rep.reshape(1).astype(jnp.int32)
    table = slot_blocks.reshape(reps, fsdp, slots)
    mine = table // block_cols == f // strips
    pos = jnp.sum(jnp.where(mine, table % block_cols, 0), axis=(0, 2)).astype(jnp.int32)
    rows_of = (lax.dynamic_index_in_dim(table, f, 1, keepdims=False) // block_cols).astype(jnp.int32)
    right, left, over = around(1, reps), around(-1, reps), around(2, reps)

    def send(x, way):
        return lax.ppermute(x, "rep", way)

    mine_rows = grads[0]

    def rows_at(k, lo):
        return lax.dynamic_slice_in_dim(mine_rows, lax.rem(rep + k, reps) * part + lo, half, 0)

    far_r = send(rows_at(2, 0), right)
    far_l = send(rows_at(2, half), left)
    low_a = send(rows_at(1, half), right)
    top_b = send(rows_at(3, 0), left)
    top_a = send((rows_at(1, 0).astype(f32) + far_r.astype(f32)).astype(bf16), right)
    low_b = send((rows_at(3, half).astype(f32) + far_l.astype(f32)).astype(bf16), left)
    whole = pl.BlockSpec((half, columns), lambda i, pos, me: (0, 0))
    spread = pl.pallas_call(
        spread_kernel,
        out_shape=shape((fsdp, part, side)),
        grid_spec=pltpu.PrefetchScalarGridSpec(
            num_scalar_prefetch=2,
            grid=(1,),
            in_specs=[pl.BlockSpec((part, columns), lambda i, pos, me: (me[0], 0))] + [whole] * 4,
            out_specs=pl.BlockSpec((fsdp, part, side), lambda i, pos, me: (0, 0, 0)),
        ),
        compiler_params=params(16),
        cost_estimate=cost(2),
        name="spread",
    )(pos, me, mine_rows, top_a, top_b, low_a, low_b)

    arrived = lax.all_to_all(spread, "fsdp", 0, 0).reshape(-1, strips * part, side)
    piece = shape((slots, strips * part, side))
    p0, p1, p2, p3 = call(pick_kernel, [piece] * reps, (rows_of, me, arrived), [SM, SM, VM], 16, cost(2), "pick")
    g1, g2, g3 = send(p3, left), send(p2, over), send(p1, right)

    slot = (slots, side, side)
    g, moment_new, second_new, u0, u1, u2, u3 = call(
        update_kernel, [shape(slot)] * 3 + [piece] * reps,
        (me, p0, g1, g2, g3, basis_left, basis_right, moment, second), [SM] + [VM] * 8, 40, cost(10), "update_block",
        [pltpu.VMEM((side, side), bf16)])

    def per_slot(*lead):
        return pl.BlockSpec((lead[0] if lead else 1, side, side), lambda s: (s, 0, 0))

    stat_left_new, stat_right_new, power, gram = pl.pallas_call(
        stat_kernel,
        grid=(slots,),
        out_shape=[shape(slot, f32)] * 2 + [shape((2 * slots, side, side), f32)] * 2,
        in_specs=[per_slot()] * 5,
        out_specs=[per_slot()] * 2 + [per_slot(2)] * 2,
        compiler_params=params(50),
        cost_estimate=cost(15, 16 * MIB),
        name="statistics",
    )(g, basis_left, basis_right, stat_left, stat_right)
    early, gram_rest, power_rest = factor_first(gram, power)
    basis_left_new, basis_right_new = factor_last(gram_rest, power_rest, early)

    v1, v2, v3 = send(u3, left), send(u2, over), send(u1, right)
    (back,) = call(unpick_kernel, [shape((slots * reps, strips * part, side))], (rows_of, me, u0, v1, v2, v3),
                   [SM, SM] + [VM] * 4, 16, cost(2), "unpick")
    home = lax.all_to_all(back.reshape(fsdp, part, side), "fsdp", 0, 0)
    (quarter,) = call(unspread_kernel, [shape((part, columns))], (pos, home), [SM, VM], 16, cost(2), "unspread")
    from_l = send(quarter, right)
    from_r = send(quarter, left)
    over_l = send(from_l[:half], right)
    over_r = send(from_r[half:], left)
    update = jnp.zeros((rows, columns), bf16)
    for k, x in ((0, quarter), (reps - 1, from_l), (1, from_r)):
        update = lax.dynamic_update_slice_in_dim(update, x, lax.rem(rep + k, reps) * part, 0)
    for lo, x in ((0, over_l), (half, over_r)):
        update = lax.dynamic_update_slice_in_dim(update, x, lax.rem(rep + 2, reps) * part + lo, 0)
    return (update, basis_left_new, basis_right_new, stat_left_new, stat_right_new, moment_new, second_new)


def solution(mesh):
    owner = P(("rep", "fsdp"), None, None)
    return jax.shard_map(
        on_device,
        mesh=mesh,
        in_specs=(P("rep", "fsdp", None), P()) + (owner,) * 6,
        out_specs=(P("fsdp", None),) + (owner,) * 6,
        check_vma=False,
    )
```

```python
import jax
import jax.numpy as jnp
from jax import lax
from jax.experimental import pallas as pl
from jax.experimental.pallas import tpu as pltpu
from jax.sharding import PartitionSpec as P

BETA_STAT = 0.95
BETA_ONE = 0.9
BETA_TWO = 0.95
EPSILON = 1e-08
MIB = 1024 * 1024
NT = 128
PANEL = 32
SUB = 8

f32 = jnp.float32
bf16 = jnp.bfloat16
VM = pl.BlockSpec(memory_space=pltpu.VMEM)
SM = pl.BlockSpec(memory_space=pltpu.SMEM)
HBM = pl.BlockSpec(memory_space=pl.ANY)


def shape(dims, kind=bf16):
    return jax.ShapeDtypeStruct(dims, kind)


def params(limit):
    return pltpu.CompilerParams(vmem_limit_bytes=limit * MIB)


def cost(us, nbytes=MIB):
    return pl.CostEstimate(flops=int(us * 1e9), bytes_accessed=nbytes, transcendentals=0)


def around(step, size):
    return [(i, (i + step) % size) for i in range(size)]


def spread_kernel(pos, own, one, two, out):
    count, _, width = out.shape

    def move(d, _):
        at = pl.ds(pl.multiple_of(pos[d] * width, width), width)
        total = own[:, at].astype(f32) + one[:, at].astype(f32) + two[:, at].astype(f32)
        out[d] = (total * 0.25).astype(bf16)
        return 0

    lax.fori_loop(0, count, move, 0)


def pick_kernel(rows_of, me, received, *pieces):
    reps = len(pieces)
    for k in range(reps):
        for s in range(pieces[k].shape[0]):
            pieces[k][s] = received[rows_of[lax.rem(me[0] + k, reps), s]]


def unpick_kernel(rows_of, me, *refs):
    pieces, out = refs[:-1], refs[-1]
    reps = len(pieces)
    for k in range(reps):
        for s in range(pieces[k].shape[0]):
            out[rows_of[lax.rem(me[0] + k, reps), s]] = pieces[k][s]


def unspread_kernel(pos, received, top, low):
    count, rows, width = received.shape
    half = rows // 2

    def move(d, _):
        at = pl.ds(pl.multiple_of(pos[d] * width, width), width)
        top[:, at] = received[d, :half, :]
        low[:, at] = received[d, half:, :]
        return 0

    lax.fori_loop(0, count, move, 0)


def dot(a, b, left=1, right=0):
    return lax.dot_general(a, b, (((left,), (right,)), ((), ())), preferred_element_type=f32)


def update_kernel(me, *refs):
    halves, sources = (refs[0:4], refs[4:8]), refs[8:12]
    g_ref, moment_new, second_new, *outs, full, held, sem = refs[12:]
    slots = g_ref.shape[0]
    strips = 4
    part = outs[0].shape[1] // strips
    half = part // 2
    copies = [[pltpu.make_async_copy(x.at[s], held.at[n, s], sem.at[n, s]) for n, x in enumerate(sources)] for s in range(slots)]
    for s in range(slots):
        for copy in copies[s]:
            copy.start()

    def rows(k, t, low, height):
        return pl.ds(pl.multiple_of((t * 4 + lax.rem(me[0] + k, 4)) * part + low, height), height)

    for low, pieces in enumerate(halves):
        for k, piece in enumerate(pieces):
            for s in range(slots):
                for t in range(strips):
                    g_ref[s, rows(k, t, low * half, half), :] = piece[s, t * half:(t + 1) * half, :]
    for s in range(slots):
        for copy in copies[s]:
            copy.wait()
        g, bl, br = g_ref[s], held[0, s], held[1, s]
        first = (BETA_ONE * held[2, s].astype(f32) + (1.0 - BETA_ONE) * g.astype(f32)).astype(bf16)
        moment_new[s] = first
        rotated_grad = dot(dot(bl, g, 0, 0).astype(bf16), br)
        rotated_moment = dot(dot(bl, first, 0, 0).astype(bf16), br)
        wide = BETA_TWO * held[3, s].astype(f32) + (1.0 - BETA_TWO) * rotated_grad * rotated_grad
        second_new[s] = wide.astype(bf16)
        scaled = (rotated_moment / (jnp.sqrt(wide) + EPSILON)).astype(bf16)
        full[...] = dot(dot(bl, scaled).astype(bf16), br, 1, 1).astype(bf16)
        for k, out in enumerate(outs):
            for t in range(strips):
                out[s, t * part:(t + 1) * part, :] = full[rows(k, t, 0, part), :]


def split3(a):
    hi = a.astype(bf16)
    rest = a - hi.astype(f32)
    mid = rest.astype(bf16)
    return hi, mid, (rest - mid.astype(f32)).astype(bf16)


def stat_kernel(g_ref, bl_ref, br_ref, sl_ref, sr_ref, sl_new, sr_new, power, gram):
    g = g_ref[0]
    for side, (old, new, basis, axis) in enumerate(((sl_ref, sl_new, bl_ref, 1), (sr_ref, sr_new, br_ref, 0))):
        stat = BETA_STAT * old[0] + (1.0 - BETA_STAT) * dot(g, g, axis, axis)
        new[0] = stat
        hi, mid, low = split3(stat)
        b = basis[0]
        p = dot(hi, b) + (dot(mid, b) + dot(low, b))
        power[side] = p
        half = p.shape[1] // 2
        gram[side, :half, :] = exact_dot(p[:, :half], p, 0, 0)
        gram[side, half:, half:] = exact_dot(p[:, half:], p[:, half:], 0, 0)
        gram[side, half:, :half] = jnp.zeros((half, half), f32)


def lane_column(block, lane):
    return jnp.broadcast_to(block[:, lane:lane + 1], block.shape)


def row_of(block, row):
    return jnp.broadcast_to(block[row:row + 1, :], block.shape)


def inverse_factors(work, out, count):
    lane = lax.broadcasted_iota(jnp.int32, (SUB, NT), 1)
    row = lax.broadcasted_iota(jnp.int32, (SUB, NT), 0)
    every = range(count)
    tiles = PANEL // SUB
    for start in range(0, NT, PANEL):
        panel = [[work[m, start + q * SUB:start + (q + 1) * SUB, :] for q in range(tiles)] for m in every]
        for t in range(tiles):
            first = start + t * SUB
            own = (lane >= first) & (lane < first + SUB)
            unit = (lane == first + row).astype(f32)
            cols = [[lane_column(panel[m][t], first + b) for b in range(SUB)] for m in every]
            body = [jnp.where(own, unit, panel[m][t]) for m in every]
            ahead = list(body)
            pivots = [cols[m][0] for m in every]
            for b in range(SUB):
                here = row == b
                for m in every:
                    if b:
                        ahead[m] = jnp.where(here, body[m], ahead[m])
                        pivots[m] = jnp.where(here, cols[m][b], pivots[m])
                    pivot = row_of(cols[m][b], b)
                    inv = pl.reciprocal(pivot, approx=True)
                    inv = inv * (2.0 - pivot * inv)
                    scaled = jnp.where(here, -1.0, cols[m][b]) * inv
                    body[m] = jnp.where(here, 0.0, body[m]) - scaled * row_of(body[m], b)
                    for c in range(b + 1, SUB):
                        cols[m][c] = jnp.where(here, 0.0, cols[m][c]) - scaled * row_of(cols[m][c], b)
            for m in every:
                root = lax.rsqrt(pivots[m])
                out[m, first:first + SUB, :] = jnp.where(lane < first + SUB, ahead[m] * root, 0.0)
            spread = [[row_of(body[m], b) for b in range(SUB)] for m in every]
            for q in [(t + d) % tiles for d in range(1, tiles)]:
                for m in every:
                    rows = panel[m][q]
                    total = jnp.where(own, 0.0, rows)
                    for b in range(SUB):
                        total = total - lane_column(rows, first + b) * spread[m][b]
                    panel[m][q] = total
            for m in every:
                panel[m][t] = body[m]
        end = start + PANEL
        if end < NT:
            below = lax.broadcasted_iota(jnp.int32, (NT - end, NT), 1)
            own = (below >= start) & (below < end)
            for m in every:
                rows = work[m, end:, :]
                done = jnp.concatenate(panel[m], axis=0)
                work[m, end:, :] = jnp.where(own, 0.0, rows) - exact_dot(rows[:, start:end], done)


def exact_dot(a, b, left=1, right=0):
    return lax.dot_general(
        a, b, (((left,), (right,)), ((), ())), precision=lax.Precision.HIGHEST, preferred_element_type=f32
    )


def split2(a):
    hi = a.astype(bf16)
    return hi, (a - hi.astype(f32)).astype(bf16)


def close_dot(a, b, left=1, right=0):
    (a_hi, a_lo), (b_hi, b_lo) = split2(a), split2(b)
    return dot(a_hi, b_hi, left, right) + (dot(a_hi, b_lo, left, right) + dot(a_lo, b_hi, left, right))


def factor_kernel(steps, a_hbm, p_hbm, *refs):
    count, side, _ = a_hbm.shape
    rows = p_hbm.shape[1]
    done_side = steps * NT
    last = done_side == side
    *refs, a, p, work, inv, sem = refs
    if last:
        *early, left_out, right_out = refs
    else:
        x_out, a_out, p_out = refs
    corner = pltpu.make_async_copy(a_hbm.at[:, :NT, :NT], work, sem.at[0])
    rest = [pltpu.make_async_copy(a_hbm, a, sem.at[1]), pltpu.make_async_copy(p_hbm, p, sem.at[2])]
    corner.start()
    for copy in rest:
        copy.start()
    done = 0
    if last:
        for x in early:
            for m in range(count):
                (left_out, right_out)[m % 2][m // 2, :, done:done + x.shape[2]] = x[m]
            done += x.shape[2]
    corner.wait()

    def step(k, _):
        @pl.when(k > 0)
        def _():
            at = pl.multiple_of(k * NT, NT)
            for m in range(count):
                work[m] = a[m, pl.ds(at, NT), pl.ds(at, NT)]

        inverse_factors(work, inv, count)

        @pl.when(k == 0)
        def _():
            for copy in rest:
                copy.wait()

        for kk in range(steps):

            @pl.when(k == kk)
            def _():
                lo, hi = kk * NT, (kk + 1) * NT
                for m in range(count):
                    w = inv[m]
                    x = close_dot(p[m, :, lo:hi], w, 1, 1)
                    if last:
                        (left_out, right_out)[m % 2][m // 2, :, done + lo:done + hi] = x.astype(bf16)
                    else:
                        x_out[m, :, lo:hi] = x.astype(bf16)
                    if hi < side:
                        u = exact_dot(w, a[m, lo:hi, hi:])
                        for r in range(0, side - hi, NT):
                            fresh = a[m, hi + r:hi + r + NT, hi + r:] - exact_dot(u[:, r:r + NT], u[:, r:], 0, 0)
                            if hi == done_side:
                                a_out[m, r:r + NT, r:] = fresh
                            else:
                                a[m, hi + r:hi + r + NT, hi + r:] = fresh
                        fresh = p[m, :, hi:] - close_dot(x, u)
                        if hi == done_side:
                            p_out[m] = fresh
                        else:
                            p[m, :, hi:] = fresh

        return 0

    if steps == 1:
        step(jnp.int32(0), 0)
    else:
        lax.fori_loop(0, steps, step, 0)


def factor(steps, a, p, early, name, us):
    count, side, _ = a.shape
    rows = p.shape[1]
    rest = side - steps * NT
    if rest:
        outs = [shape((count, rows, steps * NT)), shape((count, rest, rest), f32), shape((count, rows, rest), f32)]
    else:
        outs = [shape((count // 2, rows, rows))] * 2
    scratch = [pltpu.VMEM((count, side, side), f32), pltpu.VMEM((count, rows, side), f32)]
    scratch += [pltpu.VMEM((count, NT, NT), f32)] * 2 + [pltpu.SemaphoreType.DMA((3,))]
    return call(lambda *refs: factor_kernel(steps, *refs), outs, (a, p, *early), [HBM, HBM] + [VM] * len(early), 58,
                cost(us, 12 * MIB), name, scratch)

def call(kernel, outs, ins, specs, limit, est, name, scratch=(), out_specs=None, **extra):
    return pl.pallas_call(
        kernel,
        out_shape=outs,
        in_specs=specs,
        out_specs=out_specs or [VM] * len(outs),
        scratch_shapes=list(scratch),
        compiler_params=params(limit),
        cost_estimate=est,
        name=name,
        **extra,
    )(*ins)


def on_device(grads, slot_blocks, basis_left, basis_right, stat_left, stat_right, moment, second):
    fsdp = lax.axis_size("fsdp")
    reps = lax.axis_size("rep")
    slots, side, _ = basis_left.shape
    _, rows, columns = grads.shape
    block_cols = columns // side
    strips = side // rows
    part = rows // reps
    half = part // 2
    f = lax.axis_index("fsdp")
    rep = lax.axis_index("rep")
    me = rep.reshape(1).astype(jnp.int32)
    table = slot_blocks.reshape(reps, fsdp, slots)
    mine = table // block_cols == f // strips
    pos = jnp.sum(jnp.where(mine, table % block_cols, 0), axis=(0, 2)).astype(jnp.int32)
    rows_of = (lax.dynamic_index_in_dim(table, f, 1, keepdims=False) // block_cols).astype(jnp.int32)
    right, left, over = around(1, reps), around(-1, reps), around(2, reps)

    def send(x, way):
        return lax.ppermute(x, "rep", way)

    mine_rows = grads[0]

    def rows_at(source, k, low):
        return lax.dynamic_slice_in_dim(source, lax.rem(rep + k, reps) * part + low, half, 0)

    def add(x, y):
        return (x.astype(f32) + y.astype(f32)).astype(bf16)

    strip_half = shape((half, columns))
    piece = shape((slots, strips * half, side))

    def to_owners(own, one, two):
        (spread,) = call(spread_kernel, [shape((fsdp, half, side))], (pos, own, one, two), [SM] + [VM] * 3, 16, cost(2),
                         "spread")
        arrived = lax.all_to_all(spread, "fsdp", 0, 0).reshape(-1, strips * half, side)
        p0, p1, p2, p3 = call(pick_kernel, [piece] * reps, (rows_of, me, arrived), [SM, SM, VM], 16, cost(1), "pick")
        return p0, send(p3, left), send(p2, over), send(p1, right)

    across_r, direct = rows_at(mine_rows, 2, 0), rows_at(mine_rows, 3, 0)
    across_r, direct, later = lax.optimization_barrier((across_r, direct, mine_rows))
    far_r = send(across_r, right)
    top_b = send(direct, left)
    across_l, near_r, own_top = rows_at(later, 2, half), rows_at(later, 1, 0), rows_at(later, 0, 0)
    top_b, across_l = lax.optimization_barrier((top_b, across_l))
    far_l = send(across_l, left)
    top_a = send(add(near_r, far_r), right)
    low_r, low_l, own_low = rows_at(later, 1, half), rows_at(later, 3, half), rows_at(later, 0, half)
    top_a, far_l, low_r = lax.optimization_barrier((top_a, far_l, low_r))
    low_a = send(low_r, right)
    low_b = send(add(low_l, far_l), left)
    tops = to_owners(own_top, top_a, top_b)
    lows = to_owners(own_low, low_a, low_b)

    slot = (slots, side, side)

    def per_slot(height, lead=1):
        return pl.BlockSpec((lead, height, side), lambda s: (s, 0, 0))

    block = per_slot(side)
    back_piece = shape((slots, strips * part, side))
    g, moment_new, second_new, u0, u1, u2, u3 = call(
        update_kernel, [shape(slot)] * 3 + [back_piece] * reps,
        (me, *tops, *lows, basis_left, basis_right, moment, second), [SM] + [VM] * (2 * reps) + [HBM] * 4, 24, cost(6),
        "update_block",
        [pltpu.VMEM((side, side), bf16), pltpu.VMEM((4, *slot), bf16), pltpu.SemaphoreType.DMA((4, slots))])

    v1, v2, v3 = send(u3, left), send(u2, over), send(u1, right)
    stat_left_new, stat_right_new, power, gram = pl.pallas_call(
        stat_kernel,
        grid=(slots,),
        out_shape=[shape(slot, f32)] * 2 + [shape((2 * slots, side, side), f32)] * 2,
        in_specs=[block] * 5,
        out_specs=[block] * 2 + [per_slot(side, 2)] * 2,
        compiler_params=params(58),
        cost_estimate=cost(15, 16 * MIB),
        name="statistics",
    )(g, basis_left, basis_right, stat_left, stat_right)
    (back,) = call(unpick_kernel, [shape((slots * reps, strips * part, side))], (rows_of, me, u0, v1, v2, v3),
                   [SM, SM] + [VM] * 4, 16, cost(2), "unpick")
    gram, back = lax.optimization_barrier((gram, back))
    home = lax.all_to_all(back.reshape(fsdp, part, side), "fsdp", 0, 0)
    first, gram, power = factor(2, gram, power, (), "factor_upper", 18)
    top, low = call(unspread_kernel, [strip_half] * 2, (pos, home), [SM, VM], 16, cost(2), "unspread")
    gram, top, low = lax.optimization_barrier((gram, top, low))
    top_l, low_r = send(top, right), send(low, left)
    low_l, top_r = send(low, right), send(top, left)
    basis_left_new, basis_right_new = factor(2, gram, power, (first,), "factor_lower", 16)
    top_o, low_o = send(top_l, right), send(low_r, left)
    update = jnp.zeros((rows, columns), bf16)
    for x, k, at in (
        (top, 0, 0), (low, 0, half), (top_l, 3, 0), (low_l, 3, half), (top_r, 1, 0), (low_r, 1, half),
        (top_o, 2, 0), (low_o, 2, half),
    ):
        update = lax.dynamic_update_slice_in_dim(update, x, lax.rem(rep + k, reps) * part + at, 0)
    return (update, basis_left_new, basis_right_new, stat_left_new, stat_right_new, moment_new, second_new)


def solution(mesh):
    owner = P(("rep", "fsdp"), None, None)
    return jax.shard_map(
        on_device,
        mesh=mesh,
        in_specs=(P("rep", "fsdp", None), P()) + (owner,) * 6,
        out_specs=(P("fsdp", None),) + (owner,) * 6,
        check_vma=False,
    )
```

```python
import jax
import jax.numpy as jnp
from jax import lax
from jax.experimental import pallas as pl
from jax.experimental.pallas import tpu as pltpu
from jax.sharding import PartitionSpec as P

BETA_STAT = 0.95
BETA_ONE = 0.9
BETA_TWO = 0.95
EPSILON = 1e-08
MIB = 1024 * 1024
NT = 128
PANEL = 32
SUB = 8

f32 = jnp.float32
bf16 = jnp.bfloat16
VM = pl.BlockSpec(memory_space=pltpu.VMEM)
SM = pl.BlockSpec(memory_space=pltpu.SMEM)
HBM = pl.BlockSpec(memory_space=pl.ANY)


def shape(dims, kind=bf16):
    return jax.ShapeDtypeStruct(dims, kind)


def params(limit):
    return pltpu.CompilerParams(vmem_limit_bytes=limit * MIB)


def cost(us, nbytes=MIB):
    return pl.CostEstimate(flops=int(us * 1e9), bytes_accessed=nbytes, transcendentals=0)


def around(step, size):
    return [(i, (i + step) % size) for i in range(size)]


def spread_kernel(pos, own, one, two, out):
    count, _, width = out.shape

    def move(d, _):
        at = pl.ds(pl.multiple_of(pos[d] * width, width), width)
        total = own[:, at].astype(f32) + one[:, at].astype(f32) + two[:, at].astype(f32)
        out[d] = (total * 0.25).astype(bf16)
        return 0

    lax.fori_loop(0, count, move, 0)


def pick_kernel(rows_of, me, received, *pieces):
    reps = len(pieces)
    for k in range(reps):
        for s in range(pieces[k].shape[0]):
            pieces[k][s] = received[rows_of[lax.rem(me[0] + k, reps), s]]


def unpick_kernel(rows_of, received, out):
    for k in range(received.shape[0]):
        for s in range(received.shape[1]):
            out[rows_of[k, s]] = received[k, s]


def unspread_kernel(pos, received, top, low):
    count, rows, width = received.shape
    half = rows // 2

    def move(d, _):
        at = pl.ds(pl.multiple_of(pos[d] * width, width), width)
        top[:, at] = received[d, :half, :]
        low[:, at] = received[d, half:, :]
        return 0

    lax.fori_loop(0, count, move, 0)


def dot(a, b, left=1, right=0):
    return lax.dot_general(a, b, (((left,), (right,)), ((), ())), preferred_element_type=f32)


def update_kernel(me, *refs):
    halves, sources = (refs[0:4], refs[4:8]), refs[8:12]
    g_ref, moment_new, second_new, out, full, held, sem = refs[12:]
    slots = g_ref.shape[0]
    strips = 4
    part = out.shape[2] // strips
    half = part // 2
    for s in range(slots):
        for n, x in enumerate(sources):
            pltpu.make_async_copy(x.at[s], held.at[n, s], sem.at[n, s]).start()

    def rows(k, t, low, height):
        return pl.ds(pl.multiple_of((t * 4 + lax.rem(me[0] + k, 4)) * part + low, height), height)

    def one_slot(s, _):
        for low, pieces in enumerate(halves):
            for k, piece in enumerate(pieces):
                for t in range(strips):
                    g_ref[s, rows(k, t, low * half, half), :] = piece[s, t * half:(t + 1) * half, :]
        for n, x in enumerate(sources):
            pltpu.make_async_copy(x.at[s], held.at[n, s], sem.at[n, s]).wait()
        g, bl, br = g_ref[s], held[0, s], held[1, s]
        first = (BETA_ONE * held[2, s].astype(f32) + (1.0 - BETA_ONE) * g.astype(f32)).astype(bf16)
        moment_new[s] = first
        rotated_grad = dot(dot(bl, g, 0, 0).astype(bf16), br)
        rotated_moment = dot(dot(bl, first, 0, 0).astype(bf16), br)
        wide = BETA_TWO * held[3, s].astype(f32) + (1.0 - BETA_TWO) * rotated_grad * rotated_grad
        second_new[s] = wide.astype(bf16)
        scaled = (rotated_moment / (jnp.sqrt(wide) + EPSILON)).astype(bf16)
        full[...] = dot(dot(bl, scaled).astype(bf16), br, 1, 1).astype(bf16)
        for t in range(strips):
            for k in range(4):
                at = (t * 4 + k) * part
                out[k, s, t * part:(t + 1) * part, :] = full[at:at + part, :]
        return 0

    lax.fori_loop(0, slots, one_slot, 0)


def split3(a):
    hi = a.astype(bf16)
    rest = a - hi.astype(f32)
    mid = rest.astype(bf16)
    return hi, mid, (rest - mid.astype(f32)).astype(bf16)


def stat_kernel(g_ref, bl_ref, br_ref, sl_ref, sr_ref, sl_new, sr_new, power, gram, stat, basis):
    g = g_ref[0]
    for side, (old, new, turn, axis) in enumerate(((sl_ref, sl_new, bl_ref, 1), (sr_ref, sr_new, br_ref, 0))):
        fresh = BETA_STAT * old[0] + (1.0 - BETA_STAT) * dot(g, g, axis, axis)
        new[0] = fresh
        stat[side] = fresh
        basis[side] = turn[0]

    def one_side(side, _):
        hi, mid, low = split3(stat[side])
        b = basis[side]
        p = dot(hi, b) + (dot(mid, b) + dot(low, b))
        power[side] = p
        half = p.shape[1] // 2
        gram[side, :half, :] = exact_dot(p[:, :half], p, 0, 0)
        gram[side, half:, half:] = exact_dot(p[:, half:], p[:, half:], 0, 0)
        gram[side, half:, :half] = jnp.zeros((half, half), f32)
        return 0

    lax.fori_loop(0, 2, one_side, 0)


def lane_column(block, lane):
    return jnp.broadcast_to(block[:, lane:lane + 1], block.shape)


def row_of(block, row):
    return jnp.broadcast_to(block[row:row + 1, :], block.shape)


def inverse_factors(work, out, count):
    lane = lax.broadcasted_iota(jnp.int32, (SUB, NT), 1)
    row = lax.broadcasted_iota(jnp.int32, (SUB, NT), 0)
    every = range(count)
    tiles = PANEL // SUB
    for start in range(0, NT, PANEL):
        panel = [[work[m, start + q * SUB:start + (q + 1) * SUB, :] for q in range(tiles)] for m in every]
        for t in range(tiles):
            first = start + t * SUB
            own = (lane >= first) & (lane < first + SUB)
            unit = (lane == first + row).astype(f32)
            cols = [[lane_column(panel[m][t], first + b) for b in range(SUB)] for m in every]
            body = [jnp.where(own, unit, panel[m][t]) for m in every]
            ahead = list(body)
            pivots = [cols[m][0] for m in every]
            for b in range(SUB):
                here = row == b
                for m in every:
                    if b:
                        ahead[m] = jnp.where(here, body[m], ahead[m])
                        pivots[m] = jnp.where(here, cols[m][b], pivots[m])
                    pivot = row_of(cols[m][b], b)
                    inv = pl.reciprocal(pivot, approx=True)
                    inv = inv * (2.0 - pivot * inv)
                    scaled = jnp.where(here, -1.0, cols[m][b]) * inv
                    body[m] = jnp.where(here, 0.0, body[m]) - scaled * row_of(body[m], b)
                    for c in range(b + 1, SUB):
                        cols[m][c] = jnp.where(here, 0.0, cols[m][c]) - scaled * row_of(cols[m][c], b)
            for m in every:
                root = lax.rsqrt(pivots[m])
                out[m, first:first + SUB, :] = jnp.where(lane < first + SUB, ahead[m] * root, 0.0)
            spread = [[row_of(body[m], b) for b in range(SUB)] for m in every]
            for q in [(t + d) % tiles for d in range(1, tiles)]:
                for m in every:
                    rows = panel[m][q]
                    total = jnp.where(own, 0.0, rows)
                    for b in range(SUB):
                        total = total - lane_column(rows, first + b) * spread[m][b]
                    panel[m][q] = total
            for m in every:
                panel[m][t] = body[m]
        end = start + PANEL
        if end < NT:
            below = lax.broadcasted_iota(jnp.int32, (NT - end, NT), 1)
            own = (below >= start) & (below < end)
            for m in every:
                rows = work[m, end:, :]
                done = jnp.concatenate(panel[m], axis=0)
                work[m, end:, :] = jnp.where(own, 0.0, rows) - exact_dot(rows[:, start:end], done)


def exact_dot(a, b, left=1, right=0):
    return lax.dot_general(
        a, b, (((left,), (right,)), ((), ())), precision=lax.Precision.HIGHEST, preferred_element_type=f32
    )


def split2(a):
    hi = a.astype(bf16)
    return hi, (a - hi.astype(f32)).astype(bf16)


def close_dot(a, b, left=1, right=0):
    (a_hi, a_lo), (b_hi, b_lo) = split2(a), split2(b)
    return dot(a_hi, b_hi, left, right) + (dot(a_hi, b_lo, left, right) + dot(a_lo, b_hi, left, right))


def factor_kernel(steps, a_hbm, p_hbm, *refs):
    count, side, _ = a_hbm.shape
    rows = p_hbm.shape[1]
    done_side = steps * NT
    last = done_side == side
    *refs, a, p, work, inv, sem = refs
    if last:
        *early, left_out, right_out = refs
    else:
        x_out, a_out, p_out = refs
    corner = pltpu.make_async_copy(a_hbm.at[:, :NT, :NT], work, sem.at[0])
    rest = [pltpu.make_async_copy(a_hbm, a, sem.at[1]), pltpu.make_async_copy(p_hbm, p, sem.at[2])]
    corner.start()
    for copy in rest:
        copy.start()
    done = 0
    if last:
        for x in early:
            for m in range(count):
                (left_out, right_out)[m % 2][m // 2, :, done:done + x.shape[2]] = x[m]
            done += x.shape[2]
    corner.wait()

    def step(k, _):
        @pl.when(k > 0)
        def _():
            at = pl.multiple_of(k * NT, NT)
            for m in range(count):
                work[m] = a[m, pl.ds(at, NT), pl.ds(at, NT)]

        inverse_factors(work, inv, count)

        @pl.when(k == 0)
        def _():
            for copy in rest:
                copy.wait()

        for kk in range(steps):

            @pl.when(k == kk)
            def _():
                lo, hi = kk * NT, (kk + 1) * NT
                for m in range(count):
                    w = inv[m]
                    x = close_dot(p[m, :, lo:hi], w, 1, 1)
                    if last:
                        (left_out, right_out)[m % 2][m // 2, :, done + lo:done + hi] = x.astype(bf16)
                    else:
                        x_out[m, :, lo:hi] = x.astype(bf16)
                    if hi < side:
                        u = exact_dot(w, a[m, lo:hi, hi:])
                        for r in range(0, side - hi, NT):
                            fresh = a[m, hi + r:hi + r + NT, hi + r:] - exact_dot(u[:, r:r + NT], u[:, r:], 0, 0)
                            if hi == done_side:
                                a_out[m, r:r + NT, r:] = fresh
                            else:
                                a[m, hi + r:hi + r + NT, hi + r:] = fresh
                        fresh = p[m, :, hi:] - close_dot(x, u)
                        if hi == done_side:
                            p_out[m] = fresh
                        else:
                            p[m, :, hi:] = fresh

        return 0

    if steps == 1:
        step(jnp.int32(0), 0)
    else:
        lax.fori_loop(0, steps, step, 0)


def factor(steps, a, p, early, name, us):
    count, side, _ = a.shape
    rows = p.shape[1]
    rest = side - steps * NT
    if rest:
        outs = [shape((count, rows, steps * NT)), shape((count, rest, rest), f32), shape((count, rows, rest), f32)]
    else:
        outs = [shape((count // 2, rows, rows))] * 2
    scratch = [pltpu.VMEM((count, side, side), f32), pltpu.VMEM((count, rows, side), f32)]
    scratch += [pltpu.VMEM((count, NT, NT), f32)] * 2 + [pltpu.SemaphoreType.DMA((3,))]
    return call(lambda *refs: factor_kernel(steps, *refs), outs, (a, p, *early), [HBM, HBM] + [VM] * len(early), 50,
                cost(us, 12 * MIB), name, scratch)

def call(kernel, outs, ins, specs, limit, est, name, scratch=(), out_specs=None, **extra):
    return pl.pallas_call(
        kernel,
        out_shape=outs,
        in_specs=specs,
        out_specs=out_specs or [VM] * len(outs),
        scratch_shapes=list(scratch),
        compiler_params=params(limit),
        cost_estimate=est,
        name=name,
        **extra,
    )(*ins)


def on_device(grads, slot_blocks, basis_left, basis_right, stat_left, stat_right, moment, second):
    fsdp = lax.axis_size("fsdp")
    reps = lax.axis_size("rep")
    slots, side, _ = basis_left.shape
    _, rows, columns = grads.shape
    block_cols = columns // side
    strips = side // rows
    part = rows // reps
    half = part // 2
    f = lax.axis_index("fsdp")
    rep = lax.axis_index("rep")
    me = rep.reshape(1).astype(jnp.int32)
    table = slot_blocks.reshape(reps, fsdp, slots)
    mine = table // block_cols == f // strips
    pos = jnp.sum(jnp.where(mine, table % block_cols, 0), axis=(0, 2)).astype(jnp.int32)
    rows_of = (lax.dynamic_index_in_dim(table, f, 1, keepdims=False) // block_cols).astype(jnp.int32)
    right, left, over = around(1, reps), around(-1, reps), around(2, reps)

    def send(x, way):
        return lax.ppermute(x, "rep", way)

    mine_rows = grads[0]

    def rows_at(source, k, low):
        return lax.dynamic_slice_in_dim(source, lax.rem(rep + k, reps) * part + low, half, 0)

    def add(x, y):
        return (x.astype(f32) + y.astype(f32)).astype(bf16)

    strip_half = shape((half, columns))
    piece = shape((slots, strips * half, side))

    def to_owners(own, one, two):
        (spread,) = call(spread_kernel, [shape((fsdp, half, side))], (pos, own, one, two), [SM] + [VM] * 3, 16, cost(2),
                         "spread")
        arrived = lax.all_to_all(spread, "fsdp", 0, 0).reshape(-1, strips * half, side)
        p0, p1, p2, p3 = call(pick_kernel, [piece] * reps, (rows_of, me, arrived), [SM, SM, VM], 16, cost(1), "pick")
        return p0, send(p3, left), send(p2, over), send(p1, right)

    across_r, direct = rows_at(mine_rows, 2, 0), rows_at(mine_rows, 3, 0)
    across_r, direct, later = lax.optimization_barrier((across_r, direct, mine_rows))
    far_r = send(across_r, right)
    top_b = send(direct, left)
    across_l, near_r, own_top = rows_at(later, 2, half), rows_at(later, 1, 0), rows_at(later, 0, 0)
    far_l = send(across_l, left)
    top_a = send(add(near_r, far_r), right)
    low_r, low_l, own_low = rows_at(later, 1, half), rows_at(later, 3, half), rows_at(later, 0, half)
    top_a, far_l, low_r = lax.optimization_barrier((top_a, far_l, low_r))
    low_a = send(low_r, right)
    low_b = send(add(low_l, far_l), left)
    tops = to_owners(own_top, top_a, top_b)
    lows = to_owners(own_low, low_a, low_b)

    slot = (slots, side, side)

    def per_slot(height, lead=1):
        return pl.BlockSpec((lead, height, side), lambda s: (s, 0, 0))

    block = per_slot(side)
    g, moment_new, second_new, quarters = call(
        update_kernel, [shape(slot)] * 3 + [shape((reps, slots, strips * part, side))],
        (me, *tops, *lows, basis_left, basis_right, moment, second), [SM] + [VM] * (2 * reps) + [HBM] * 4, 50, cost(6),
        "update_block",
        [pltpu.VMEM((side, side), bf16), pltpu.VMEM((4, *slot), bf16), pltpu.SemaphoreType.DMA((4, slots))])

    returned = lax.all_to_all(quarters, "rep", 0, 0)
    stat_left_new, stat_right_new, power, gram = pl.pallas_call(
        stat_kernel,
        grid=(slots,),
        out_shape=[shape(slot, f32)] * 2 + [shape((2 * slots, side, side), f32)] * 2,
        in_specs=[block] * 5,
        out_specs=[block] * 2 + [per_slot(side, 2)] * 2,
        scratch_shapes=[pltpu.VMEM((2, side, side), f32), pltpu.VMEM((2, side, side), bf16)],
        compiler_params=params(50),
        cost_estimate=cost(15, 16 * MIB),
        name="statistics",
    )(g, basis_left, basis_right, stat_left, stat_right)
    (back,) = call(unpick_kernel, [shape((slots * reps, strips * part, side))], (rows_of, returned),
                   [SM, VM], 16, cost(2), "unpick")
    gram, back = lax.optimization_barrier((gram, back))
    home = lax.all_to_all(back.reshape(fsdp, part, side), "fsdp", 0, 0)
    first, gram, power = factor(2, gram, power, (), "factor_upper", 18)
    top, low = call(unspread_kernel, [strip_half] * 2, (pos, home), [SM, VM], 16, cost(2), "unspread")
    gram, top, low = lax.optimization_barrier((gram, top, low))
    top_l, low_r = send(top, right), send(low, left)
    low_l, top_r = send(low, right), send(top, left)
    basis_left_new, basis_right_new = factor(2, gram, power, (first,), "factor_lower", 16)
    top_o, low_o = send(top_l, right), send(low_r, left)
    update = jnp.zeros((rows, columns), bf16)
    for x, k, at in (
        (top, 0, 0), (low, 0, half), (top_l, 3, 0), (low_l, 3, half), (top_r, 1, 0), (low_r, 1, half),
        (top_o, 2, 0), (low_o, 2, half),
    ):
        update = lax.dynamic_update_slice_in_dim(update, x, lax.rem(rep + k, reps) * part + at, 0)
    return (update, basis_left_new, basis_right_new, stat_left_new, stat_right_new, moment_new, second_new)


def solution(mesh):
    owner = P(("rep", "fsdp"), None, None)
    return jax.shard_map(
        on_device,
        mesh=mesh,
        in_specs=(P("rep", "fsdp", None), P()) + (owner,) * 6,
        out_specs=(P("fsdp", None),) + (owner,) * 6,
        check_vma=False,
    )
```
